32 devices in a mesh: ex: 16 (over z, x, core), feat: 2 (over y).
Axes of the slice: x: 2, y: 2, z: 4, core: 2. Of those that a mesh axis runs over, the one named last changes fastest.
Arguments:
- features: bfloat16 [1536, 8192], P('ex', 'feat'), may hold values from -100 to 100
Outputs:
- kernel: float32 [1536, 1536], P('ex', 'feat')
The draws below stay inside these ranges and needn't reach their ends.
All inputs are finite; a program needn't handle non-finite values.
Results may differ from the reference program's by a relative error of at most 0.0003.
Values may be sent and summed in bfloat16 or wider, within the bound.
A program may use at most 64 MiB of HBM per device.

```python
import jax
import jax.numpy as jnp
from jax import lax

FEAT = 8192
EXAMPLES = 1536


def draw_features(key, part):
    key = jax.random.fold_in(key, 11)
    keys = jax.random.split(key, 5)
    cluster_count = 16
    labels = jax.random.randint(keys[0], (EXAMPLES,), 0, cluster_count)
    row_scale = jnp.exp(jax.random.uniform(keys[1], (EXAMPLES,), jnp.float32, 0.0, 2.302585))
    col_scale = jnp.exp(jax.random.uniform(keys[2], (FEAT,), jnp.float32, 0.0, 2.302585))
    shared = jnp.clip(jax.random.normal(keys[3], (cluster_count, FEAT), jnp.float32), -5.0, 5.0)
    noise = jnp.clip(jax.random.normal(keys[4], (EXAMPLES, FEAT), jnp.float32), -5.0, 5.0)
    mixed = noise + 0.8 * shared[labels]
    values = 0.1 * row_scale[:, None] * col_scale[None, :] * mixed
    return values.astype(jnp.bfloat16)


def setup_inputs(seed: int = 0) -> dict:
    seeds = jax.random.split(jax.random.key(seed), 2)
    features = draw_features(jax.random.fold_in(seeds[1], 71), 0)
    return dict(features=features)


def reference(features):
    values = features.astype(jnp.float32)
    gram = jnp.dot(values, values.T, precision=lax.Precision.HIGHEST, preferred_element_type=jnp.float32)
    squares = lax.optimization_barrier(jnp.sum(values * values, axis=1)) + 1e-06
    scale = lax.rsqrt(squares)
    return gram * scale[:, None] * scale[None, :]
```

```python
import jax
import jax.numpy as jnp
from jax import lax
from jax.experimental import pallas as pl
from jax.experimental.pallas import tpu as pltpu
from jax.sharding import PartitionSpec as P

MESH = pl.DeviceIdType.MESH
EPS = 1e-06
DEPTH_STEP = 1024
STAT_ROWS = 8


def inner_tile(left, right):
    return lax.dot_general(
        left, right, (((1,), (1,)), ((), ())), preferred_element_type=jnp.float32
    )


def lane_squares(block):
    depth = block.shape[-1]
    total = None
    for start in range(0, depth, 128):
        value = block[:, start : start + 128].astype(jnp.float32)
        total = value * value if total is None else total + value * value
    return total


def hub_kernel(
    f_ref, o_ref, near, far, rows, tiles, landed, squares, send, recv, tile_send, tile_recv, local
):
    n, depth = f_ref.shape
    e, y = lax.axis_index("ex"), lax.axis_index("feat")
    z, x, c = e // 4, (e // 2) % 2, e % 2
    h = z // 2
    ox, oc, oy, oh = 1 - x, 1 - c, 1 - y, 1 - h
    hub_z, end_z = 1 + h, 3 * h
    far_hub_z, far_end_z = 1 + oh, 3 * oh
    is_hub = z == hub_z

    def at(z_, x_, c_):
        return z_ * 4 + x_ * 2 + c_

    def remote(src, dst, number, to, to_y):
        return pltpu.make_async_remote_copy(
            src_ref=src,
            dst_ref=dst,
            send_sem=send.at[number],
            recv_sem=recv.at[number],
            device_id=(to, to_y),
            device_id_type=MESH,
        )

    barrier = pltpu.get_barrier_semaphore()

    def greet(i, carry):
        to, to_y = 8 * h + i // 2, i % 2

        @pl.when(jnp.logical_or(to != e, to_y != y))
        def _():
            pl.semaphore_signal(barrier, inc=1, device_id=(to, to_y), device_id_type=MESH)

        return carry

    lax.fori_loop(0, 16, greet, 0)
    pl.semaphore_signal(
        barrier, inc=1, device_id=(at(far_hub_z, x, c), y), device_id_type=MESH
    )

    @pl.when(is_hub)
    def _():
        pl.semaphore_signal(
            barrier, inc=1, device_id=(at(far_end_z, x, c), y), device_id_type=MESH
        )
        pl.semaphore_wait(barrier, 17)

    @pl.when(jnp.logical_not(is_hub))
    def _():
        pl.semaphore_wait(barrier, 16)

    near_end = remote(f_ref, near.at[h], 0, at(hub_z, x, c), y)
    far_end = remote(f_ref, far.at[h], 2, at(far_hub_z, x, c), y)
    far_hub = remote(f_ref, far.at[oh], 1, at(far_hub_z, x, c), y)
    swap_squares = remote(squares.at[0], squares.at[1], 9, e, oy)

    def send_squares():
        own = jnp.sum(lane_squares(f_ref[...]), axis=1, keepdims=True)
        squares[0] = jnp.broadcast_to(own, (n, 128))
        swap_squares.start()

    @pl.when(jnp.logical_not(is_hub))
    def _():
        near_end.start()
        send_squares()
        near_end.wait_send()
        far_end.start()
        far_end.wait_send()

    def multiply(kind, columns, first, last):
        count = last - first
        for step in range(depth // DEPTH_STEP):
            piece = pl.ds(step * DEPTH_STEP, DEPTH_STEP)
            left = rows[first:last, :, piece].reshape(count * n, DEPTH_STEP)
            right = columns[:, :, piece].reshape(2 * n, DEPTH_STEP)
            product = inner_tile(left, right).reshape(count, n, 2 * n)
            if step == 0:
                tiles[kind, first:last, 0:n, :] = product
            else:
                tiles[kind, first:last, 0:n, :] += product

    def column_squares(kind, columns):
        lanes = lane_squares(columns[...].reshape(2 * n, depth))
        total = jnp.sum(jnp.transpose(lanes), axis=0, keepdims=True)
        tiles[kind, :, n : n + STAT_ROWS, :] = jnp.broadcast_to(
            total[None], (8, STAT_ROWS, 2 * n)
        )

    def tile_copy(kind, r, to, to_y):
        return pltpu.make_async_remote_copy(
            src_ref=tiles.at[kind, r],
            dst_ref=landed.at[y, x, c],
            send_sem=tile_send.at[kind, r],
            recv_sem=tile_recv.at[y, x, c],
            device_id=(to, to_y),
            device_id_type=MESH,
        )

    def own_tile(kind, r):
        return pltpu.make_async_copy(
            tiles.at[kind, r], landed.at[y, x, c], tile_recv.at[y, x, c]
        )

    def deliver(kind, first, last):
        to_y = h if kind == 0 else oh

        def one(r, carry):
            to_z = jnp.where((r // 2) % 2 == 0, hub_z, end_z)
            to = at(to_z, jnp.where(r // 4 == 0, x, ox), r % 2)
            mine = jnp.logical_and(to == e, to_y == y)

            @pl.when(mine)
            def _():
                own_tile(kind, r).start()

            @pl.when(jnp.logical_not(mine))
            def _():
                tile_copy(kind, r, to, to_y).start()

            return carry

        lax.fori_loop(first, last, one, 0)

    def drain(kind):
        to_y = h if kind == 0 else oh

        def one(r, carry):
            mine = jnp.logical_and(r == c, to_y == y)

            @pl.when(jnp.logical_not(mine))
            def _():
                tile_copy(kind, r, e, oy).wait_send()

            return carry

        lax.fori_loop(0, 8, one, 0)

    @pl.when(is_hub)
    def _():
        to_x = at(hub_z, ox, c)
        to_core = at(hub_z, x, oc)
        hub_to_x = remote(f_ref, rows.at[4 + c], 3, to_x, y)
        hub_to_core = remote(f_ref, rows.at[c], 5, to_core, y)
        end_to_x = remote(near.at[h], rows.at[6 + c], 4, to_x, y)
        end_to_core = remote(near.at[h], rows.at[2 + c], 6, to_core, y)
        other_hub_to_core = remote(rows.at[4 + c], rows.at[4 + c], 7, to_core, y)
        other_end_to_core = remote(rows.at[6 + c], rows.at[6 + c], 8, to_core, y)
        from_core = [
            remote(rows.at[2 * i + oc], rows.at[2 * i + oc], 5 + i, to_core, y)
            for i in range(4)
        ]
        far_hub.start()
        hub_to_x.start()
        hub_to_core.start()
        keep = [
            pltpu.make_async_copy(f_ref, near.at[oh], local.at[0]),
            pltpu.make_async_copy(f_ref, rows.at[c], local.at[1]),
            pltpu.make_async_copy(near.at[h], rows.at[2 + c], local.at[2]),
        ]
        keep[0].start()
        keep[1].start()
        send_squares()
        near_end.wait_recv()
        end_to_x.start()
        end_to_core.start()
        keep[2].start()
        hub_to_x.wait_recv()
        other_hub_to_core.start()
        for copy in keep:
            copy.wait()
        column_squares(0, near)
        from_core[0].wait_recv()
        from_core[1].wait_recv()
        from_core[2].wait_recv()
        multiply(0, near, 0, 6)
        deliver(0, 0, 6)
        end_to_x.wait_recv()
        other_end_to_core.start()
        far_hub.wait_recv()
        far_end.wait_recv()
        from_core[3].wait_recv()
        column_squares(1, far)
        multiply(1, far, 0, 8)
        deliver(1, 0, 8)
        multiply(0, near, 6, 8)
        deliver(0, 6, 8)
        for copy in (
            far_hub, hub_to_x, hub_to_core, end_to_x, end_to_core,
            other_hub_to_core, other_end_to_core,
        ):
            copy.wait_send()

    swap_squares.wait()
    row_scale = lax.rsqrt(squares[0][:, 0:1] + squares[1][:, 0:1] + EPS)
    for x_ in range(2):
        for c_ in range(2):
            for y_ in range(2):
                pltpu.make_async_copy(
                    landed.at[y_, x_, c_], landed.at[y_, x_, c_], tile_recv.at[y_, x_, c_]
                ).wait()
            total = landed[0, x_, c_] + landed[1, x_, c_]
            column_scale = lax.rsqrt(total[n : n + 1] + EPS)
            o_ref[2 * x_ + c_] = total[0:n] * row_scale * column_scale

    @pl.when(is_hub)
    def _():
        drain(0)
        drain(1)


def hub_shards(features):
    n, depth = features.shape
    pieces = pl.pallas_call(
        hub_kernel,
        out_shape=jax.ShapeDtypeStruct((4, n, 2 * n), jnp.float32),
        in_specs=[pl.BlockSpec(memory_space=pltpu.VMEM)],
        out_specs=pl.BlockSpec(memory_space=pltpu.VMEM),
        scratch_shapes=[
            pltpu.VMEM((2, n, depth), jnp.bfloat16),
            pltpu.VMEM((2, n, depth), jnp.bfloat16),
            pltpu.VMEM((8, n, depth), jnp.bfloat16),
            pltpu.VMEM((2, 8, n + STAT_ROWS, 2 * n), jnp.float32),
            pltpu.VMEM((2, 2, 2, n + STAT_ROWS, 2 * n), jnp.float32),
            pltpu.VMEM((2, n, 128), jnp.float32),
            pltpu.SemaphoreType.DMA((10,)),
            pltpu.SemaphoreType.DMA((10,)),
            pltpu.SemaphoreType.DMA((2, 8)),
            pltpu.SemaphoreType.DMA((2, 2, 2)),
            pltpu.SemaphoreType.DMA((3,)),
        ],
        compiler_params=pltpu.CompilerParams(
            collective_id=0, has_side_effects=True, vmem_limit_bytes=40 * 1024 * 1024
        ),
        name="hub_gram",
    )(features)
    pieces = pieces.reshape(2, 2, n, 2, n)
    return jnp.transpose(pieces, (2, 3, 0, 1, 4)).reshape(n, 8 * n)


def gathered_shards(features):
    local_squares = jnp.sum(jnp.square(features.astype(jnp.float32)), axis=1)
    row_norms = lax.psum(local_squares, "feat")
    every_norm = lax.all_gather(row_norms, "ex", axis=0, tiled=True)
    partial_gram = inner_tile(features, lax.all_gather(features, "ex", axis=0, tiled=True))
    gram = lax.psum_scatter(partial_gram, "feat", scatter_dimension=1, tiled=True)
    col_width = gram.shape[1]
    col_norms = lax.dynamic_slice_in_dim(
        every_norm, lax.axis_index("feat") * col_width, col_width, 0
    )
    row_scale = lax.rsqrt(row_norms + EPS)
    col_scale = lax.rsqrt(col_norms + EPS)
    return gram * row_scale[:, None] * col_scale[None, :]


def solution(mesh):
    four_groups = mesh.shape["ex"] == 16 and mesh.shape["feat"] == 2
    shards = hub_shards if four_groups else gathered_shards
    return jax.shard_map(
        shards,
        mesh=mesh,
        in_specs=(P("ex", "feat"),),
        out_specs=P("ex", "feat"),
        check_vma=False,
    )
```

```python
import jax
import jax.numpy as jnp
from jax import lax
from jax.experimental import pallas as pl
from jax.experimental.pallas import tpu as pltpu
from jax.sharding import PartitionSpec as P

MESH = pl.DeviceIdType.MESH
EPS = 1e-06
DEPTH_STEP = 1024
STAT_ROWS = 8
PIECES = 4


def inner_tile(left, right):
    return lax.dot_general(
        left, right, (((1,), (1,)), ((), ())), preferred_element_type=jnp.float32
    )


def lane_squares(block):
    depth = block.shape[-1]
    total = None
    for start in range(0, depth, 128):
        value = block[:, start : start + 128].astype(jnp.float32)
        total = value * value if total is None else total + value * value
    return total


def fold(block, pad):
    n = block.shape[0]
    kept = n - pad
    free = 128 - n
    tail = block[kept:n]
    extra = [tail[:, i * free : (i + 1) * free] for i in range(n // free)]
    return jnp.concatenate([block[0:kept], jnp.concatenate(extra, axis=0)], axis=1)


def unfold(folded, pad):
    n = folded.shape[0] + pad
    free = 128 - n
    extra = folded[:, n:128]
    tail = [extra[i * pad : (i + 1) * pad] for i in range(n // free)]
    return jnp.concatenate([folded[:, 0:n], jnp.concatenate(tail, axis=1)], axis=0)


def hub_kernel(
    f_ref, o_ref, cols, rows, acc, tiles, landed, squares, send, recv, tile_send, tile_recv, local
):
    n, depth = f_ref.shape
    pad = n * (128 - n) // 128
    kept = n - pad
    e, y = lax.axis_index("ex"), lax.axis_index("feat")
    z, x, c = e // 4, (e // 2) % 2, e % 2
    h = z // 2
    ox, oc, oy, oh = 1 - x, 1 - c, 1 - y, 1 - h
    hub_z, end_z = 1 + h, 3 * h
    far_hub_z, far_end_z = 1 + oh, 3 * oh
    is_hub = z == hub_z
    width = depth // PIECES

    def at(z_, x_, c_):
        return z_ * 4 + x_ * 2 + c_

    def remote(src, dst, number, to, to_y):
        return pltpu.make_async_remote_copy(
            src_ref=src,
            dst_ref=dst,
            send_sem=send.at[number],
            recv_sem=recv.at[number],
            device_id=(to, to_y),
            device_id_type=MESH,
        )

    def remote_pieces(src, dst, number, to, to_y):
        return [
            remote(
                src.at[:, pl.ds(k * width, width)],
                dst.at[:, pl.ds(k * width, width)],
                number + k,
                to,
                to_y,
            )
            for k in range(PIECES)
        ]

    own = pltpu.make_async_copy(f_ref, cols.at[1], local.at[0])
    own.start()

    barrier = pltpu.get_barrier_semaphore()

    def greet(i, carry):
        to, to_y = 8 * h + i // 2, i % 2

        @pl.when(jnp.logical_or(to != e, to_y != y))
        def _():
            pl.semaphore_signal(barrier, inc=1, device_id=(to, to_y), device_id_type=MESH)

        return carry

    lax.fori_loop(0, 16, greet, 0)
    pl.semaphore_signal(
        barrier, inc=1, device_id=(at(far_hub_z, x, c), y), device_id_type=MESH
    )

    @pl.when(is_hub)
    def _():
        pl.semaphore_signal(
            barrier, inc=1, device_id=(at(far_end_z, x, c), y), device_id_type=MESH
        )
        pl.semaphore_wait(barrier, 17)

    @pl.when(jnp.logical_not(is_hub))
    def _():
        pl.semaphore_wait(barrier, 16)

    near_end = remote(f_ref, cols.at[0], 0, at(hub_z, x, c), y)
    far_hub = remote(f_ref, cols.at[2], 1, at(far_hub_z, x, c), y)
    far_end = remote_pieces(f_ref, cols.at[3], 8, at(far_hub_z, x, c), y)
    swap_squares = remote(squares.at[0], squares.at[1], 2, e, oy)

    def send_squares():
        own.wait()
        total = jnp.sum(lane_squares(cols[1]), axis=1, keepdims=True)
        squares[0] = jnp.broadcast_to(total, (n, 128))
        swap_squares.start()

    @pl.when(jnp.logical_not(is_hub))
    def _():
        near_end.start()
        send_squares()
        near_end.wait_send()
        for copy in far_end:
            copy.start()
        for copy in far_end:
            copy.wait_send()

    def multiply(j, first, last, start, size, fresh):
        count = last - first
        for step in range(size // DEPTH_STEP):
            piece = pl.ds(start + step * DEPTH_STEP, DEPTH_STEP)
            left = rows[first:last, :, piece].reshape(count * n, DEPTH_STEP)
            product = inner_tile(left, cols[j, :, piece]).reshape(count, n, n)
            if fresh and step == 0:
                acc[j, first:last] = product
            else:
                acc[j, first:last] += product

    def column_squares(j):
        lanes = lane_squares(cols[j])
        total = jnp.sum(jnp.transpose(lanes), axis=0, keepdims=True)
        tiles[j, :, kept : kept + STAT_ROWS, 0:n] = jnp.broadcast_to(
            total[None], (8, STAT_ROWS, n)
        )

    def tile_copy(j, r, to, to_y, group):
        return pltpu.make_async_remote_copy(
            src_ref=tiles.at[j, r],
            dst_ref=landed.at[y, x, c, group],
            send_sem=tile_send.at[j, r],
            recv_sem=tile_recv.at[y, x, c, group],
            device_id=(to, to_y),
            device_id_type=MESH,
        )

    def place(j):
        to_y = h if j < 2 else oh
        group = h if j in (0, 2) else oh
        return to_y, group

    def deliver(j, first, last):
        to_y, group = place(j)

        def one(r, carry):
            tiles[j, r, 0:kept, :] = fold(acc[j, r], pad)
            to_z = jnp.where((r // 2) % 2 == 0, hub_z, end_z)
            to = at(to_z, jnp.where(r // 4 == 0, x, ox), r % 2)
            mine = jnp.logical_and(to == e, to_y == y)

            @pl.when(mine)
            def _():
                pltpu.make_async_copy(
                    tiles.at[j, r], landed.at[y, x, c, group], tile_recv.at[y, x, c, group]
                ).start()

            @pl.when(jnp.logical_not(mine))
            def _():
                tile_copy(j, r, to, to_y, group).start()

            return carry

        lax.fori_loop(first, last, one, 0)

    def drain(j):
        to_y, group = place(j)

        def one(r, carry):
            mine = jnp.logical_and(r == c, to_y == y)

            @pl.when(jnp.logical_not(mine))
            def _():
                tile_copy(j, r, e, oy, group).wait_send()

            return carry

        lax.fori_loop(0, 8, one, 0)

    @pl.when(is_hub)
    def _():
        to_x = at(hub_z, ox, c)
        to_core = at(hub_z, x, oc)
        hub_to_x = remote(f_ref, rows.at[4 + c], 3, to_x, y)
        hub_to_core = remote(f_ref, rows.at[c], 4, to_core, y)
        end_to_core = remote(cols.at[0], rows.at[2 + c], 5, to_core, y)
        other_hub_to_core = remote(rows.at[4 + c], rows.at[4 + c], 6, to_core, y)
        end_to_x = remote_pieces(cols.at[0], rows.at[6 + c], 12, to_x, y)
        other_end_to_core = remote_pieces(rows.at[6 + c], rows.at[6 + c], 16, to_core, y)
        from_core = [
            remote(rows.at[2 * i + oc], rows.at[2 * i + oc], 4 + i, to_core, y)
            for i in range(3)
        ]
        last_from_core = remote_pieces(rows.at[6 + oc], rows.at[6 + oc], 16, to_core, y)
        far_hub.start()
        hub_to_x.start()
        hub_to_core.start()
        keep = [
            pltpu.make_async_copy(f_ref, rows.at[c], local.at[1]),
            pltpu.make_async_copy(cols.at[0], rows.at[2 + c], local.at[2]),
        ]
        keep[0].start()
        send_squares()
        column_squares(1)
        near_end.wait_recv()
        for copy in end_to_x:
            copy.start()
        end_to_core.start()
        keep[1].start()
        hub_to_x.wait_recv()
        other_hub_to_core.start()
        column_squares(0)
        for copy in keep:
            copy.wait()
        for copy in from_core:
            copy.wait_recv()
        multiply(1, 0, 6, 0, depth, True)
        deliver(1, 0, 6)
        multiply(0, 0, 6, 0, depth, True)
        deliver(0, 0, 6)
        far_hub.wait_recv()
        column_squares(2)
        multiply(2, 0, 6, 0, depth, True)
        deliver(2, 0, 6)
        for k in range(PIECES):
            end_to_x[k].wait_recv()
            other_end_to_core[k].start()
            far_end[k].wait_recv()
            multiply(3, 0, 6, k * width, width, k == 0)
            if k == PIECES - 1:
                column_squares(3)
                deliver(3, 0, 6)
            last_from_core[k].wait_recv()
            for j in range(4):
                multiply(j, 6, 8, k * width, width, k == 0)
        for j in range(4):
            deliver(j, 6, 8)
        for copy in [far_hub, hub_to_x, hub_to_core, end_to_core, other_hub_to_core]:
            copy.wait_send()
        for copy in end_to_x + other_end_to_core:
            copy.wait_send()

    swap_squares.wait()
    row_scale = lax.rsqrt(squares[0][:, 0:1] + squares[1][:, 0:1] + EPS)
    for x_ in range(2):
        for c_ in range(2):
            for g_ in range(2):
                for y_ in range(2):
                    pltpu.make_async_copy(
                        landed.at[y_, x_, c_, g_],
                        landed.at[y_, x_, c_, g_],
                        tile_recv.at[y_, x_, c_, g_],
                    ).wait()
                total = landed[0, x_, c_, g_] + landed[1, x_, c_, g_]
                column_scale = lax.rsqrt(total[kept : kept + 1, 0:n] + EPS)
                o_ref[4 * g_ + 2 * x_ + c_] = (
                    unfold(total[0:kept], pad) * row_scale * column_scale
                )

    @pl.when(is_hub)
    def _():
        for j in range(4):
            drain(j)


def hub_shards(features):
    n, depth = features.shape
    kept = n - n * (128 - n) // 128
    pieces = pl.pallas_call(
        hub_kernel,
        out_shape=jax.ShapeDtypeStruct((8, n, n), jnp.float32),
        in_specs=[pl.BlockSpec(memory_space=pl.ANY)],
        out_specs=pl.BlockSpec(memory_space=pltpu.VMEM),
        scratch_shapes=[
            pltpu.VMEM((4, n, depth), jnp.bfloat16),
            pltpu.VMEM((8, n, depth), jnp.bfloat16),
            pltpu.VMEM((4, 8, n, n), jnp.float32),
            pltpu.VMEM((4, 8, kept + STAT_ROWS, 128), jnp.float32),
            pltpu.VMEM((2, 2, 2, 2, kept + STAT_ROWS, 128), jnp.float32),
            pltpu.VMEM((2, n, 128), jnp.float32),
            pltpu.SemaphoreType.DMA((20,)),
            pltpu.SemaphoreType.DMA((20,)),
            pltpu.SemaphoreType.DMA((4, 8)),
            pltpu.SemaphoreType.DMA((2, 2, 2, 2)),
            pltpu.SemaphoreType.DMA((3,)),
        ],
        compiler_params=pltpu.CompilerParams(
            collective_id=0, has_side_effects=True, vmem_limit_bytes=50 * 1024 * 1024
        ),
        name="hub_gram",
    )(features)
    return jnp.transpose(pieces, (1, 0, 2)).reshape(n, 8 * n)


def gathered_shards(features):
    local_squares = jnp.sum(jnp.square(features.astype(jnp.float32)), axis=1)
    row_norms = lax.psum(local_squares, "feat")
    every_norm = lax.all_gather(row_norms, "ex", axis=0, tiled=True)
    partial_gram = inner_tile(features, lax.all_gather(features, "ex", axis=0, tiled=True))
    gram = lax.psum_scatter(partial_gram, "feat", scatter_dimension=1, tiled=True)
    col_width = gram.shape[1]
    col_norms = lax.dynamic_slice_in_dim(
        every_norm, lax.axis_index("feat") * col_width, col_width, 0
    )
    row_scale = lax.rsqrt(row_norms + EPS)
    col_scale = lax.rsqrt(col_norms + EPS)
    return gram * row_scale[:, None] * col_scale[None, :]


def solution(mesh):
    four_groups = mesh.shape["ex"] == 16 and mesh.shape["feat"] == 2
    shards = hub_shards if four_groups else gathered_shards
    return jax.shard_map(
        shards,
        mesh=mesh,
        in_specs=(P("ex", "feat"),),
        out_specs=P("ex", "feat"),
        check_vma=False,
    )
```

```python
import jax
import jax.numpy as jnp
from jax import lax
from jax.experimental import pallas as pl
from jax.experimental.pallas import tpu as pltpu
from jax.sharding import PartitionSpec as P

MESH = pl.DeviceIdType.MESH
EPS = 1e-06
DEPTH_STEP = 1024
STAT_ROWS = 8
PIECES = 4


def inner_tile(left, right):
    return lax.dot_general(
        left, right, (((1,), (1,)), ((), ())), preferred_element_type=jnp.float32
    )


def lane_squares(block):
    depth = block.shape[-1]
    total = None
    for start in range(0, depth, 128):
        value = block[:, start : start + 128].astype(jnp.float32)
        total = value * value if total is None else total + value * value
    return total


def fold(block, pad):
    n = block.shape[0]
    kept = n - pad
    free = 128 - n
    tail = block[kept:n]
    extra = [tail[:, i * free : (i + 1) * free] for i in range(n // free)]
    return jnp.concatenate([block[0:kept], jnp.concatenate(extra, axis=0)], axis=1)


def unfold(folded, pad):
    n = folded.shape[0] + pad
    free = 128 - n
    extra = folded[:, n:128]
    tail = [extra[i * pad : (i + 1) * pad] for i in range(n // free)]
    return jnp.concatenate([folded[:, 0:n], jnp.concatenate(tail, axis=1)], axis=0)


def hub_kernel(
    f_ref, o_ref, cols, rows, acc, tiles, landed, squares, send, recv, tile_send, tile_recv, local
):
    n, depth = f_ref.shape
    pad = n * (128 - n) // 128
    kept = n - pad
    e, y = lax.axis_index("ex"), lax.axis_index("feat")
    z, x, c = e // 4, (e // 2) % 2, e % 2
    h = z // 2
    ox, oc, oy, oh = 1 - x, 1 - c, 1 - y, 1 - h
    hub_z, end_z = 1 + h, 3 * h
    far_hub_z, far_end_z = 1 + oh, 3 * oh
    is_hub = z == hub_z
    width = depth // PIECES

    def at(z_, x_, c_):
        return z_ * 4 + x_ * 2 + c_

    def remote(src, dst, number, to, to_y):
        return pltpu.make_async_remote_copy(
            src_ref=src,
            dst_ref=dst,
            send_sem=send.at[number],
            recv_sem=recv.at[number],
            device_id=(to, to_y),
            device_id_type=MESH,
        )

    def remote_pieces(src, dst, number, to, to_y):
        return [
            remote(
                src.at[:, pl.ds(k * width, width)],
                dst.at[:, pl.ds(k * width, width)],
                number + k,
                to,
                to_y,
            )
            for k in range(PIECES)
        ]

    own = pltpu.make_async_copy(f_ref, cols.at[1], local.at[0])
    own.start()

    barrier = pltpu.get_barrier_semaphore()

    def greet(i, carry):
        to, to_y = 8 * h + i // 2, i % 2

        @pl.when(jnp.logical_or(to != e, to_y != y))
        def _():
            pl.semaphore_signal(barrier, inc=1, device_id=(to, to_y), device_id_type=MESH)

        return carry

    lax.fori_loop(0, 16, greet, 0)
    pl.semaphore_signal(
        barrier, inc=1, device_id=(at(far_hub_z, x, c), y), device_id_type=MESH
    )

    @pl.when(is_hub)
    def _():
        pl.semaphore_signal(
            barrier, inc=1, device_id=(at(far_end_z, x, c), y), device_id_type=MESH
        )
        pl.semaphore_wait(barrier, 17)

    @pl.when(jnp.logical_not(is_hub))
    def _():
        pl.semaphore_wait(barrier, 16)

    near_end = remote(f_ref, cols.at[0], 0, at(hub_z, x, c), y)
    far_hub = remote(f_ref, cols.at[2], 1, at(far_hub_z, x, c), y)
    far_end = remote_pieces(f_ref, cols.at[3], 8, at(far_hub_z, x, c), y)
    swap_squares = remote(squares.at[0], squares.at[1], 2, e, oy)

    def send_squares():
        own.wait()
        total = jnp.sum(lane_squares(cols[1]), axis=1, keepdims=True)
        squares[0] = jnp.broadcast_to(total, (n, 128))
        swap_squares.start()

    @pl.when(jnp.logical_not(is_hub))
    def _():
        near_end.start()
        send_squares()
        near_end.wait_send()
        for copy in far_end:
            copy.start()
        for copy in far_end:
            copy.wait_send()

    def multiply(j, first, last, start, size, fresh):
        count = last - first
        for step in range(size // DEPTH_STEP):
            piece = pl.ds(start + step * DEPTH_STEP, DEPTH_STEP)
            left = rows[first:last, :, piece].reshape(count * n, DEPTH_STEP)
            product = inner_tile(left, cols[j, :, piece]).reshape(count, n, n)
            if fresh and step == 0:
                acc[j, first:last] = product
            else:
                acc[j, first:last] += product

    def across(block):
        total = jnp.sum(jnp.transpose(lane_squares(block)), axis=0, keepdims=True)
        return jnp.broadcast_to(total, (STAT_ROWS, n))

    def column_squares(j):
        total = across(cols[j])
        count = 4 if j < 2 else 8
        tiles[j, 0:count, kept : kept + STAT_ROWS, 0:n] = jnp.broadcast_to(
            total[None], (count, STAT_ROWS, n)
        )

    def row_squares(r):
        total = across(rows[r])
        tiles[0, r, kept : kept + STAT_ROWS, 0:n] = total
        tiles[1, r, kept : kept + STAT_ROWS, 0:n] = total

    def tile_copy(j, r, to, to_y, group):
        return pltpu.make_async_remote_copy(
            src_ref=tiles.at[j, r],
            dst_ref=landed.at[y, x, c, group],
            send_sem=tile_send.at[j, r],
            recv_sem=tile_recv.at[y, x, c, group],
            device_id=(to, to_y),
            device_id_type=MESH,
        )

    def place(j):
        to_y = h if j < 2 else oh
        group = h if j in (0, 2) else oh
        return to_y, group

    def deliver(j, first, last):
        to_y, group = place(j)

        def one(r, carry):
            tiles[j, r, 0:kept, :] = fold(acc[j, r], pad)
            to_z = jnp.where((r // 2) % 2 == 0, hub_z, end_z)
            to = at(to_z, jnp.where(r // 4 == 0, x, ox), r % 2)
            mine = jnp.logical_and(to == e, to_y == y)

            @pl.when(mine)
            def _():
                pltpu.make_async_copy(
                    tiles.at[j, r], landed.at[y, x, c, group], tile_recv.at[y, x, c, group]
                ).start()

            @pl.when(jnp.logical_not(mine))
            def _():
                tile_copy(j, r, to, to_y, group).start()

            return carry

        lax.fori_loop(first, last, one, 0)

    def turned_copy(j, r, to, to_y):
        from_c = r % 2
        group = oh if r < 6 else h
        return pltpu.make_async_remote_copy(
            src_ref=tiles.at[j, r],
            dst_ref=landed.at[y, ox, from_c, group],
            send_sem=tile_send.at[j, r],
            recv_sem=tile_recv.at[y, ox, from_c, group],
            device_id=(to, to_y),
            device_id_type=MESH,
        )

    def deliver_turned(j, r):
        tiles[j, r, 0:kept, :] = fold(jnp.transpose(acc[j, r]), pad)
        if j == 0:
            turned_copy(j, r, at(end_z, x, c), h).start()
            return
        from_c = r % 2
        group = oh if r < 6 else h

        @pl.when(h == y)
        def _():
            pltpu.make_async_copy(
                tiles.at[j, r],
                landed.at[y, ox, from_c, group],
                tile_recv.at[y, ox, from_c, group],
            ).start()

        @pl.when(h != y)
        def _():
            turned_copy(j, r, e, h).start()

    def drain_turned():
        for r in range(4, 8):
            turned_copy(0, r, e, oy).wait_send()

            @pl.when(h != y)
            def _():
                turned_copy(1, r, e, oy).wait_send()

    def drain(j):
        to_y, group = place(j)

        def one(r, carry):
            mine = jnp.logical_and(r == c, to_y == y)

            @pl.when(jnp.logical_not(mine))
            def _():
                tile_copy(j, r, e, oy, group).wait_send()

            return carry

        lax.fori_loop(0, 4 if j < 2 else 8, one, 0)

    @pl.when(is_hub)
    def _():
        to_x = at(hub_z, ox, c)
        to_core = at(hub_z, x, oc)
        hub_to_x = remote(f_ref, rows.at[4 + c], 3, to_x, y)
        hub_to_core = remote(f_ref, rows.at[c], 4, to_core, y)
        end_to_core = remote(cols.at[0], rows.at[2 + c], 5, to_core, y)
        other_hub_to_core = remote(rows.at[4 + c], rows.at[4 + c], 6, to_core, y)
        end_to_x = remote_pieces(cols.at[0], rows.at[6 + c], 12, to_x, y)
        other_end_to_core = remote_pieces(rows.at[6 + c], rows.at[6 + c], 16, to_core, y)
        from_core = [
            remote(rows.at[2 * i + oc], rows.at[2 * i + oc], 4 + i, to_core, y)
            for i in range(3)
        ]
        last_from_core = remote_pieces(rows.at[6 + oc], rows.at[6 + oc], 16, to_core, y)
        far_hub.start()
        hub_to_x.start()
        hub_to_core.start()
        keep = [
            pltpu.make_async_copy(f_ref, rows.at[c], local.at[1]),
            pltpu.make_async_copy(cols.at[0], rows.at[2 + c], local.at[2]),
        ]
        keep[0].start()
        send_squares()
        column_squares(1)
        near_end.wait_recv()
        for copy in end_to_x:
            copy.start()
        end_to_core.start()
        keep[1].start()
        hub_to_x.wait_recv()
        other_hub_to_core.start()
        column_squares(0)
        for copy in keep:
            copy.wait()
        for copy in from_core:
            copy.wait_recv()
        multiply(1, 0, 6, 0, depth, True)
        deliver(1, 0, 4)
        multiply(0, 0, 6, 0, depth, True)
        deliver(0, 0, 4)
        for r in (4, 5):
            row_squares(r)
            deliver_turned(0, r)
            deliver_turned(1, r)
        far_hub.wait_recv()
        column_squares(2)
        multiply(2, 0, 6, 0, depth, True)
        deliver(2, 0, 6)
        for k in range(PIECES):
            end_to_x[k].wait_recv()
            other_end_to_core[k].start()
            far_end[k].wait_recv()
            multiply(3, 0, 6, k * width, width, k == 0)
            if k == PIECES - 1:
                column_squares(3)
                deliver(3, 0, 6)
            last_from_core[k].wait_recv()
            for j in range(4):
                multiply(j, 6, 8, k * width, width, k == 0)
        deliver(3, 6, 8)
        deliver(2, 6, 8)
        for r in (6, 7):
            row_squares(r)
            deliver_turned(0, r)
            deliver_turned(1, r)
        for copy in [far_hub, hub_to_x, hub_to_core, end_to_core, other_hub_to_core]:
            copy.wait_send()
        for copy in end_to_x + other_end_to_core:
            copy.wait_send()

    swap_squares.wait()
    row_scale = lax.rsqrt(squares[0][:, 0:1] + squares[1][:, 0:1] + EPS)
    for x_ in range(2):
        for c_ in range(2):
            for g_ in range(2):
                for y_ in range(2):
                    pltpu.make_async_copy(
                        landed.at[y_, x_, c_, g_],
                        landed.at[y_, x_, c_, g_],
                        tile_recv.at[y_, x_, c_, g_],
                    ).wait()
                total = landed[0, x_, c_, g_] + landed[1, x_, c_, g_]
                column_scale = lax.rsqrt(total[kept : kept + 1, 0:n] + EPS)
                o_ref[4 * g_ + 2 * x_ + c_] = (
                    unfold(total[0:kept], pad) * row_scale * column_scale
                )

    @pl.when(is_hub)
    def _():
        for j in range(4):
            drain(j)
        drain_turned()


def hub_shards(features):
    n, depth = features.shape
    kept = n - n * (128 - n) // 128
    pieces = pl.pallas_call(
        hub_kernel,
        out_shape=jax.ShapeDtypeStruct((8, n, n), jnp.float32),
        in_specs=[pl.BlockSpec(memory_space=pl.ANY)],
        out_specs=pl.BlockSpec(memory_space=pltpu.VMEM),
        scratch_shapes=[
            pltpu.VMEM((4, n, depth), jnp.bfloat16),
            pltpu.VMEM((8, n, depth), jnp.bfloat16),
            pltpu.VMEM((4, 8, n, n), jnp.float32),
            pltpu.VMEM((4, 8, kept + STAT_ROWS, 128), jnp.float32),
            pltpu.VMEM((2, 2, 2, 2, kept + STAT_ROWS, 128), jnp.float32),
            pltpu.VMEM((2, n, 128), jnp.float32),
            pltpu.SemaphoreType.DMA((20,)),
            pltpu.SemaphoreType.DMA((20,)),
            pltpu.SemaphoreType.DMA((4, 8)),
            pltpu.SemaphoreType.DMA((2, 2, 2, 2)),
            pltpu.SemaphoreType.DMA((3,)),
        ],
        compiler_params=pltpu.CompilerParams(
            collective_id=0, has_side_effects=True, vmem_limit_bytes=62 * 1024 * 1024
        ),
        name="hub_gram",
    )(features)
    return jnp.transpose(pieces, (1, 0, 2)).reshape(n, 8 * n)


def gathered_shards(features):
    local_squares = jnp.sum(jnp.square(features.astype(jnp.float32)), axis=1)
    row_norms = lax.psum(local_squares, "feat")
    every_norm = lax.all_gather(row_norms, "ex", axis=0, tiled=True)
    partial_gram = inner_tile(features, lax.all_gather(features, "ex", axis=0, tiled=True))
    gram = lax.psum_scatter(partial_gram, "feat", scatter_dimension=1, tiled=True)
    col_width = gram.shape[1]
    col_norms = lax.dynamic_slice_in_dim(
        every_norm, lax.axis_index("feat") * col_width, col_width, 0
    )
    row_scale = lax.rsqrt(row_norms + EPS)
    col_scale = lax.rsqrt(col_norms + EPS)
    return gram * row_scale[:, None] * col_scale[None, :]


def solution(mesh):
    four_groups = mesh.shape["ex"] == 16 and mesh.shape["feat"] == 2
    shards = hub_shards if four_groups else gathered_shards
    return jax.shard_map(
        shards,
        mesh=mesh,
        in_specs=(P("ex", "feat"),),
        out_specs=P("ex", "feat"),
        check_vma=False,
    )
```
